256 devices in a mesh: dp: 32 (over x, y, core), seq: 8 (over z).
Axes of the slice: x: 4, y: 4, z: 8, core: 2. Of those that a mesh axis runs over, the one named last changes fastest.
Arguments:
- latents: bfloat16 [224, 8, 64, 1152], P('dp', 'seq'), may hold values from -7 to 7
- w_spatial_qkv: bfloat16 [1152, 1728], replicated, may hold values from -1 to 1
- w_spatial_out: bfloat16 [576, 1152], replicated, may hold values from -0.25 to 0.25
- w_temporal_qkv: bfloat16 [1152, 1728], replicated, may hold values from -1 to 1
- w_temporal_out: bfloat16 [576, 1152], replicated, may hold values from -0.25 to 0.25
- spatial_len: int32 [224], replicated, may hold values from 16 to 64, as said below
- frames_len: int32 [224], replicated, may hold values from 1 to 8
- target: int32 [224], replicated, may hold values from 0 to 223, as said below
Outputs:
- blended: bfloat16 [224, 8, 64, 1152], P('dp', 'seq')
The draws below stay inside these ranges and needn't reach their ends.
Inputs may be any that keep to these rules, and one draw needn't show every extreme that they name: `spatial_len`: each clip's bucket holds 16, 32, 48 or 64 tokens. `target`: a permutation of the clip slots; clip slot c of group g goes to slot c of some group; the 7 clips of a group go to 7 different groups, so a group sends exactly one clip to each of 7 groups and receives 7 clips.
All inputs are finite; a program needn't handle non-finite values.
Results may differ from the reference program's by a relative error of at most 0.019.
Values may be sent and summed in bfloat16 or wider, within the bound.
No kernel may reach another device: no remote copies, remote signals or barrier semaphores. Data moves between devices by JAX's collectives and lax.ppermute only.
A program may use at most 128 MiB of HBM per device.

```python
import jax
import jax.numpy as jnp
from jax import lax

D = 1152
HEADS = 8
HD = 72
S_MAX = 64
CLIPS_DEV = 7
CAP = 1
HW = 576
FRAMES = 8
CLIPS = 224
N_DP = 32


def draw_latents(key, part):
    key = jax.random.fold_in(key, 5)
    subkeys = jax.random.split(key, 1)
    full_shape = (CLIPS, FRAMES, S_MAX, D)
    entries = jax.random.truncated_normal(subkeys[0], -6.0, 6.0, full_shape, jnp.float32)
    return jnp.clip(entries, -7.0, 7.0).astype(jnp.bfloat16)


def draw_w_spatial_qkv(key, part):
    key = jax.random.fold_in(key, 41)
    subkeys = jax.random.split(key, 1)
    entries = jax.random.truncated_normal(subkeys[0], -6.0, 6.0, (D, 3 * HW), jnp.float32) * D ** (-0.5)
    return jnp.clip(entries, -1.0, 1.0).astype(jnp.bfloat16)


def draw_w_temporal_qkv(key, part):
    key = jax.random.fold_in(key, 43)
    subkeys = jax.random.split(key, 1)
    entries = jax.random.truncated_normal(subkeys[0], -6.0, 6.0, (D, 3 * HW), jnp.float32) * D ** (-0.5)
    return jnp.clip(entries, -1.0, 1.0).astype(jnp.bfloat16)


def draw_spatial_len(key, part):
    key = jax.random.fold_in(key, 11)
    levels = jax.random.randint(key, (CLIPS,), 1, 5)
    sizes = levels * (S_MAX // 4)
    return sizes.at[0].set(S_MAX).at[1].set(S_MAX // 4).astype(jnp.int32)


def draw_frames_len(key, part):
    key = jax.random.fold_in(key, 23)
    counts = jax.random.randint(key, (CLIPS,), 1, FRAMES + 1)
    return counts.at[1].set(FRAMES).at[2].set(1).astype(jnp.int32)


def draw_target(key, part):
    key = jax.random.fold_in(key, 37)
    subkeys = jax.random.split(key, 2)
    order = jax.random.permutation(subkeys[0], N_DP)
    shifts = order[:CLIPS_DEV // CAP]
    relabel = jax.random.permutation(subkeys[1], N_DP).astype(jnp.int32)
    inverse = jnp.zeros((N_DP,), jnp.int32).at[relabel].set(jnp.arange(N_DP, dtype=jnp.int32))
    slot_ids = jnp.arange(CLIPS, dtype=jnp.int32)
    groups = slot_ids // CLIPS_DEV
    within = slot_ids % CLIPS_DEV
    moved = relabel[(inverse[groups] + shifts[within // CAP]) % N_DP]
    return (moved * CLIPS_DEV + within).astype(jnp.int32)


def noise(own_key, shape, scale, most, held_as=jnp.bfloat16):
    values = scale * jax.random.normal(own_key, shape, jnp.float32)
    return jnp.clip(values, min=-most, max=most).astype(held_as)


def setup_inputs(seed: int = 0) -> dict:
    seeds = jax.random.split(jax.random.key(seed), 9)
    return {
        "latents": draw_latents(jax.random.fold_in(seeds[8], 71), 0),
        "w_spatial_qkv": draw_w_spatial_qkv(jax.random.fold_in(seeds[8], 71), 0),
        "w_spatial_out": noise(seeds[2], (HW, D), HW ** -0.5, 0.25),
        "w_temporal_qkv": draw_w_temporal_qkv(jax.random.fold_in(seeds[8], 71), 0),
        "w_temporal_out": noise(seeds[4], (HW, D), HW ** -0.5, 0.25),
        "spatial_len": draw_spatial_len(jax.random.fold_in(seeds[8], 71), 0),
        "frames_len": draw_frames_len(jax.random.fold_in(seeds[8], 71), 0),
        "target": draw_target(jax.random.fold_in(seeds[8], 71), 0),
    }


def layer_norm(values):
    wide = values.astype(jnp.float32)
    centre = wide - lax.optimization_barrier(jnp.mean(wide, axis=-1, keepdims=True))
    spread = lax.optimization_barrier(jnp.mean(centre * centre, axis=-1, keepdims=True))
    return (centre * lax.rsqrt(spread + 1e-06)).astype(jnp.bfloat16)

def attend(query, keys, values, scores_form, out_form, live):
    scores = jnp.einsum(scores_form, query.astype(jnp.float32), keys.astype(jnp.float32)) * HD ** (-0.5)
    scores = jnp.where(live, scores, -1e+30)
    probs = jax.nn.softmax(scores, axis=-1).astype(jnp.bfloat16)
    return jnp.einsum(out_form, probs.astype(jnp.float32), values.astype(jnp.float32)).astype(jnp.bfloat16)

def one_clip(packed, w_spatial_qkv, w_spatial_out, w_temporal_qkv, w_temporal_out):
    clip, slen, flen = packed
    frames, slots, width = clip.shape
    normed = layer_norm(clip).reshape(-1, width)
    qkv = jnp.dot(normed, w_spatial_qkv, preferred_element_type=jnp.float32).astype(jnp.bfloat16)
    qkv = qkv.reshape(frames, slots, 3, HEADS, HD)
    live = (jnp.arange(slots) < slen)[None, None, None, :]
    attn = attend(qkv[:, :, 0], qkv[:, :, 1], qkv[:, :, 2], 'fshe,fthe->fhst', 'fhst,fthe->fshe', live)
    mid = clip.reshape(-1, width).astype(jnp.float32) + jnp.dot(attn.reshape(-1, HW), w_spatial_out, preferred_element_type=jnp.float32)
    mid = mid.astype(jnp.bfloat16)
    qkv_t = jnp.dot(layer_norm(mid), w_temporal_qkv, preferred_element_type=jnp.float32).astype(jnp.bfloat16)
    qkv_t = qkv_t.reshape(frames, slots, 3, HEADS, HD)
    live_t = (jnp.arange(frames) < flen)[None, None, None, :]
    attn_t = attend(qkv_t[:, :, 0], qkv_t[:, :, 1], qkv_t[:, :, 2], 'fshe,gshe->shfg', 'shfg,gshe->fshe', live_t)
    block = mid.astype(jnp.float32) + jnp.dot(attn_t.reshape(-1, HW), w_temporal_out, preferred_element_type=jnp.float32)
    return block.astype(jnp.bfloat16).reshape(frames, slots, width)

def reference(latents, w_spatial_qkv, w_spatial_out, w_temporal_qkv, w_temporal_out, spatial_len, frames_len, target):

    def step(packed):
        return one_clip(packed, w_spatial_qkv, w_spatial_out, w_temporal_qkv, w_temporal_out)
    blocks = lax.map(step, (latents, spatial_len, frames_len))
    inverse = jnp.argsort(target).astype(jnp.int32)
    return blocks[inverse]
```

```python
import functools

import jax
import jax.numpy as jnp
from jax import lax
from jax.experimental import pallas as pl
from jax.experimental.pallas import tpu as pltpu
from jax.sharding import PartitionSpec as P

HEADS = 8
HD = 72
HW = 576
BLOCK = 128
VMEM = 51 * 1024 * 1024
ROWS_BY_ROWS = (((1,), (1,)), ((), ()))
COLUMNS_BY_COLUMNS = (((0,), (0,)), ((), ()))
SCALE = HD ** (-0.5) * 1.4426950408889634


def layer_norm(values):
    wide = values.astype(jnp.float32)
    centre = wide - jnp.mean(wide, axis=-1, keepdims=True)
    spread = jnp.mean(centre * centre, axis=-1, keepdims=True)
    return (centre * lax.rsqrt(spread + 1e-06)).astype(jnp.bfloat16)


def dot(left, right, dims):
    return lax.dot_general(left, right, dims, preferred_element_type=jnp.float32)


def attention_part(rows, w_q, w_k, w_v, w_out, biases):
    normed = layer_norm(rows)
    query = dot(w_q(), normed, ROWS_BY_ROWS)
    keys = dot(w_k(), normed, ROWS_BY_ROWS)
    probs = []
    start = 0
    for bias in biases:
        stop = start + bias.shape[0]
        for at in range(0, HW, HD):
            scores = dot(
                keys[at : at + HD, start:stop].astype(jnp.bfloat16),
                query[at : at + HD, start:stop].astype(jnp.bfloat16),
                COLUMNS_BY_COLUMNS,
            )
            scores = scores * SCALE + bias
            weight = jnp.exp2(scores - jnp.max(scores, axis=0, keepdims=True))
            total = jnp.sum(weight, axis=0, keepdims=True)
            probs.append((weight.astype(jnp.bfloat16), 1.0 / total))
        start = stop
    values = dot(w_v(), normed, ROWS_BY_ROWS)
    attn = []
    start = 0
    for index, bias in enumerate(biases):
        stop = start + bias.shape[0]
        heads = []
        for head in range(HEADS):
            at = head * HD
            weight, share = probs[index * HEADS + head]
            part = values[at : at + HD, start:stop].astype(jnp.bfloat16)
            heads.append(jnp.dot(part, weight, preferred_element_type=jnp.float32) * share)
        attn.append(jnp.concatenate(heads, axis=0))
        start = stop
    attn = jnp.concatenate(attn, axis=1).astype(jnp.bfloat16)
    block = rows.astype(jnp.float32) + dot(attn, w_out(), COLUMNS_BY_COLUMNS)
    return block.astype(jnp.bfloat16)


def iotas(size):
    return (
        lax.broadcasted_iota(jnp.int32, (size, size), 0),
        lax.broadcasted_iota(jnp.int32, (size, size), 1),
    )


def streamed(w_qkv, w_out, proj, back, sems):
    copies = [
        pltpu.make_async_copy(w_qkv.at[pl.ds(part * HW, HW)], proj.at[part], sems.at[part])
        for part in range(3)
    ]
    copies.append(pltpu.make_async_copy(w_out, back, sems.at[3]))
    for copy in copies:
        copy.start()

    def reader(part):
        def read():
            copies[part].wait()
            return proj[part] if part < 3 else back[...]

        return read

    return [reader(part) for part in range(4)]


def spatial_kernel(clips, slots, slen, x, w_qkv, w_out, out, proj, back, sems):
    weights = streamed(w_qkv, w_out, proj, back, sems)
    group = lax.axis_index("dp")
    total = clips * slots
    biases = []
    for start in range(0, total, BLOCK):
        size = min(BLOCK, total - start)
        row, col = iotas(size)
        live = jnp.zeros((size, size), jnp.bool_)
        for clip in range(start // slots, (start + size) // slots):
            first = clip * slots - start
            live = live | (
                (col >= first)
                & (col < first + slots)
                & (row >= first)
                & (row < first + slen[group * clips + clip])
            )
        biases.append(jnp.where(live, 0.0, -1e30))
    out[:total] = attention_part(x[...], *weights, biases)
    out[total:] = jnp.zeros((out.shape[0] - total, out.shape[1]), jnp.bfloat16)


def temporal_kernel(
    clips, slots, groups, frames, each, flen, target, x, w_qkv, w_out, out, proj, back, sems
):
    weights = streamed(w_qkv, w_out, proj, back, sems)
    home = lax.axis_index("dp") * frames + lax.axis_index("seq")
    slot = jnp.minimum(home * each // slots, clips - 1)
    span = frames * each
    total = groups * span
    row, col = iotas(BLOCK)
    same = (row // span == col // span) & (row % each == col % each)
    frame = row % span // each
    owner = row // span
    biases = []
    for start in range(0, total, BLOCK):
        most = jnp.zeros((BLOCK, BLOCK), jnp.int32)
        for part in range(BLOCK // span):
            group = start // span + part
            most = jnp.where(owner == part, flen[group * clips + slot], most)
        biases.append(jnp.where(same & (frame < most), 0.0, -1e30))
    block = attention_part(x[...], *weights, biases)
    for group in range(groups):
        goal = target[group * clips + slot] // clips
        out[pl.ds(pl.multiple_of(goal * span, span), span), :] = block[
            group * span : (group + 1) * span
        ]


def per_device(
    latents,
    w_spatial_qkv,
    w_spatial_out,
    w_temporal_qkv,
    w_temporal_out,
    spatial_len,
    frames_len,
    target,
):
    clips, _, slots, width = latents.shape
    groups, frames = lax.axis_size("dp"), lax.axis_size("seq")
    devices = groups * frames
    each = -(-clips * slots // devices)
    rows = devices * each
    smem = pl.BlockSpec(memory_space=pltpu.SMEM)
    vmem = pl.BlockSpec(memory_space=pltpu.VMEM)
    hbm = pl.BlockSpec(memory_space=pl.ANY)

    def exchange(values):
        return lax.all_to_all(
            values.reshape(devices, each, width),
            ("dp", "seq"),
            split_axis=0,
            concat_axis=0,
            tiled=True,
        ).reshape(rows, width)

    def call(kernel, scalars, values, w_qkv, w_out):
        return pl.pallas_call(
            kernel,
            out_shape=jax.ShapeDtypeStruct((rows, width), jnp.bfloat16),
            in_specs=[smem] * len(scalars) + [vmem, hbm, hbm],
            out_specs=vmem,
            scratch_shapes=[
                pltpu.VMEM((3, HW, width), jnp.bfloat16),
                pltpu.VMEM((HW, width), jnp.bfloat16),
                pltpu.SemaphoreType.DMA((4,)),
            ],
            compiler_params=pltpu.CompilerParams(vmem_limit_bytes=VMEM),
        )(*scalars, values, w_qkv.T, w_out)

    mid = call(
        functools.partial(spatial_kernel, clips, slots),
        [spatial_len],
        latents.reshape(clips * slots, width),
        w_spatial_qkv,
        w_spatial_out,
    )
    block = call(
        functools.partial(temporal_kernel, clips, slots, groups, frames, each),
        [frames_len, target],
        exchange(mid),
        w_temporal_qkv,
        w_temporal_out,
    )
    return exchange(block)[: clips * slots].reshape(latents.shape)


def solution(mesh):
    return jax.shard_map(
        per_device,
        mesh=mesh,
        in_specs=(P("dp", "seq", None, None), P(), P(), P(), P(), P(), P(), P()),
        out_specs=P("dp", "seq", None, None),
        check_vma=False,
    )
```

```python
import functools

import jax
import jax.numpy as jnp
from jax import lax
from jax.experimental import pallas as pl
from jax.experimental.pallas import tpu as pltpu
from jax.sharding import PartitionSpec as P

HEADS = 8
HD = 72
HW = 576
BLOCK = 128
MIB = 1024 * 1024
ROWS_BY_ROWS = (((1,), (1,)), ((), ()))
COLUMNS_BY_COLUMNS = (((0,), (0,)), ((), ()))
SCALE = HD ** (-0.5) * 1.4426950408889634


def layer_norm(values):
    wide = values.astype(jnp.float32)
    centre = wide - jnp.mean(wide, axis=-1, keepdims=True)
    spread = jnp.mean(centre * centre, axis=-1, keepdims=True)
    return (centre * lax.rsqrt(spread + 1e-06)).astype(jnp.bfloat16)


def dot(left, right, dims):
    return lax.dot_general(left, right, dims, preferred_element_type=jnp.float32)


def attention_part(rows, w_q, w_k, w_v, w_out, biases):
    normed = layer_norm(rows)
    query = dot(w_q(), normed, ROWS_BY_ROWS)
    keys = dot(w_k(), normed, ROWS_BY_ROWS)
    probs = []
    start = 0
    for bias in biases:
        stop = start + bias.shape[0]
        for at in range(0, HW, HD):
            scores = dot(
                keys[at : at + HD, start:stop].astype(jnp.bfloat16),
                query[at : at + HD, start:stop].astype(jnp.bfloat16),
                COLUMNS_BY_COLUMNS,
            )
            scores = scores * SCALE + bias
            weight = jnp.exp2(scores - jnp.max(scores, axis=0, keepdims=True))
            total = jnp.sum(weight, axis=0, keepdims=True)
            probs.append((weight.astype(jnp.bfloat16), 1.0 / total))
        start = stop
    values = dot(w_v(), normed, ROWS_BY_ROWS)
    attn = []
    start = 0
    for index, bias in enumerate(biases):
        stop = start + bias.shape[0]
        heads = []
        for head in range(HEADS):
            at = head * HD
            weight, share = probs[index * HEADS + head]
            part = values[at : at + HD, start:stop].astype(jnp.bfloat16)
            heads.append(jnp.dot(part, weight, preferred_element_type=jnp.float32) * share)
        attn.append(jnp.concatenate(heads, axis=0))
        start = stop
    attn = jnp.concatenate(attn, axis=1).astype(jnp.bfloat16)
    block = rows.astype(jnp.float32) + dot(attn, w_out(), COLUMNS_BY_COLUMNS)
    return block.astype(jnp.bfloat16)


def iotas(size):
    return (
        lax.broadcasted_iota(jnp.int32, (size, size), 0),
        lax.broadcasted_iota(jnp.int32, (size, size), 1),
    )


def streamed(w_qkv, w_out, proj, back, sems):
    copies = [
        pltpu.make_async_copy(w_qkv.at[pl.ds(part * HW, HW)], proj.at[part], sems.at[part])
        for part in range(3)
    ]
    copies.append(pltpu.make_async_copy(w_out, back, sems.at[3]))

    def reader(part):
        def read():
            copies[part].wait()
            return proj[part] if part < 3 else back[...]

        return read

    return copies, [reader(part) for part in range(4)]


def spatial_kernel(clips, slots, slen, x, w_qkv, w_out, out, proj, back, sems, own):
    copies, weights = streamed(w_qkv, w_out, proj, back, sems)
    arrival = pltpu.make_async_copy(x, own, sems.at[4])
    arrival.start()
    copies[0].start()
    group = lax.axis_index("dp")
    total = clips * slots
    biases = []
    for start in range(0, total, BLOCK):
        size = min(BLOCK, total - start)
        row, col = iotas(size)
        live = jnp.zeros((size, size), jnp.bool_)
        for clip in range(start // slots, (start + size) // slots):
            first = clip * slots - start
            live = live | (
                (col >= first)
                & (col < first + slots)
                & (row >= first)
                & (row < first + slen[group * clips + clip])
            )
        biases.append(jnp.where(live, 0.0, -1e30))
    out[total:] = jnp.zeros((out.shape[0] - total, out.shape[1]), jnp.bfloat16)
    arrival.wait()
    for copy in copies[1:]:
        copy.start()
    out[:total] = attention_part(own[...], *weights, biases)


def temporal_kernel(
    clips, slots, groups, frames, each, flen, target, x, w_qkv, w_out, out, proj, back, sems
):
    copies, weights = streamed(w_qkv, w_out, proj, back, sems)
    for copy in copies:
        copy.start()
    home = lax.axis_index("seq") * groups + lax.axis_index("dp")
    slot = jnp.minimum(home * each // slots, clips - 1)
    plane = groups * each
    row, col = iotas(plane)
    goal = jnp.zeros((plane, plane), jnp.int32)
    most = jnp.zeros((plane, plane), jnp.int32)
    for group in range(groups):
        here = col // each == group
        goal = jnp.where(here, target[group * clips + slot] // clips, goal)
        most = jnp.where(here, flen[group * clips + slot], most)
    moved = (goal == row // each) & (row % each == col % each)
    most = jnp.sum(jnp.where(moved, most.astype(jnp.float32), 0.0), axis=1, keepdims=True)
    moved = jnp.where(moved, 1.0, 0.0).astype(jnp.bfloat16)
    planes = [
        jnp.dot(
            moved, x[frame * plane : (frame + 1) * plane], preferred_element_type=jnp.float32
        ).astype(jnp.bfloat16)
        for frame in range(frames)
    ]
    part = BLOCK // frames
    starts = range(0, plane, part)
    row, col = iotas(BLOCK)
    same = row % part == col % part
    frame = (row // part).astype(jnp.float32)
    biases = []
    for start in starts:
        live = jnp.concatenate([most[start : start + part]] * frames, axis=0)
        biases.append(jnp.where(same & (frame < live), 0.0, -1e30))
    rows = jnp.concatenate([each[start : start + part] for start in starts for each in planes])
    block = attention_part(rows, *weights, biases)
    for index, start in enumerate(starts):
        for frame in range(frames):
            at = frame * plane + start
            first = index * BLOCK + frame * part
            out[at : at + part] = block[first : first + part]


def crop_kernel(pieces, x, out, sems):
    size = out.shape[0] // pieces
    copies = [
        pltpu.make_async_copy(
            x.at[pl.ds(piece * size, size)], out.at[pl.ds(piece * size, size)], sems.at[piece]
        )
        for piece in range(pieces)
    ]
    for copy in copies:
        copy.start()
    for copy in copies:
        copy.wait()


def per_device(
    latents,
    w_spatial_qkv,
    w_spatial_out,
    w_temporal_qkv,
    w_temporal_out,
    spatial_len,
    frames_len,
    target,
):
    clips, _, slots, width = latents.shape
    groups, frames = lax.axis_size("dp"), lax.axis_size("seq")
    devices = groups * frames
    each = -(-clips * slots // devices)
    rows = devices * each
    smem = pl.BlockSpec(memory_space=pltpu.SMEM)
    vmem = pl.BlockSpec(memory_space=pltpu.VMEM)
    hbm = pl.BlockSpec(memory_space=pl.ANY)

    def exchange(values):
        return lax.all_to_all(
            values.reshape(devices, each, width),
            ("seq", "dp"),
            split_axis=0,
            concat_axis=0,
            tiled=True,
        ).reshape(rows, width)

    def call(kernel, scalars, values, w_qkv, w_out, where, limit, extra):
        return pl.pallas_call(
            kernel,
            out_shape=pltpu.VMEM((rows, width), jnp.bfloat16),
            in_specs=[smem] * len(scalars) + [where, hbm, hbm],
            out_specs=vmem,
            scratch_shapes=[
                pltpu.VMEM((3, HW, width), jnp.bfloat16),
                pltpu.VMEM((HW, width), jnp.bfloat16),
                pltpu.SemaphoreType.DMA((5,)),
                *extra,
            ],
            compiler_params=pltpu.CompilerParams(vmem_limit_bytes=limit),
        )(*scalars, values, w_qkv.T, w_out)

    mid = call(
        functools.partial(spatial_kernel, clips, slots),
        [spatial_len],
        latents.reshape(clips * slots, width),
        w_spatial_qkv,
        w_spatial_out,
        hbm,
        55 * MIB,
        [pltpu.VMEM((clips * slots, width), jnp.bfloat16)],
    )
    block = call(
        functools.partial(temporal_kernel, clips, slots, groups, frames, each),
        [frames_len, target],
        exchange(mid),
        w_temporal_qkv,
        w_temporal_out,
        vmem,
        51 * MIB,
        [],
    )
    final = pl.pallas_call(
        functools.partial(crop_kernel, clips),
        out_shape=jax.ShapeDtypeStruct((clips * slots, width), jnp.bfloat16),
        in_specs=[hbm],
        out_specs=hbm,
        scratch_shapes=[pltpu.SemaphoreType.DMA((clips,))],
        compiler_params=pltpu.CompilerParams(vmem_limit_bytes=40 * MIB),
    )(exchange(block))
    return final.reshape(latents.shape)


def solution(mesh):
    return jax.shard_map(
        per_device,
        mesh=mesh,
        in_specs=(P("dp", "seq", None, None), P(), P(), P(), P(), P(), P(), P()),
        out_specs=P("dp", "seq", None, None),
        check_vma=False,
    )
```

```python
import functools

import jax
import jax.numpy as jnp
from jax import lax
from jax.experimental import pallas as pl
from jax.experimental.pallas import tpu as pltpu
from jax.sharding import PartitionSpec as P

HEADS = 8
HD = 72
HW = 576
BLOCK = 128
MIB = 1024 * 1024
ROWS_BY_ROWS = (((1,), (1,)), ((), ()))
COLUMNS_BY_COLUMNS = (((0,), (0,)), ((), ()))
SCALE = HD ** (-0.5) * 1.4426950408889634


def layer_norm(values):
    wide = values.astype(jnp.float32)
    centre = wide - jnp.mean(wide, axis=-1, keepdims=True)
    spread = jnp.mean(centre * centre, axis=-1, keepdims=True)
    return (centre * lax.rsqrt(spread + 1e-06)).astype(jnp.bfloat16)


def dot(left, right, dims):
    return lax.dot_general(left, right, dims, preferred_element_type=jnp.float32)


def attention_part(rows, w_q, w_k, w_v, w_out, biases):
    normed = layer_norm(rows)
    query = dot(w_q(), normed, ROWS_BY_ROWS)
    keys = dot(w_k(), normed, ROWS_BY_ROWS)
    probs = []
    start = 0
    for bias in biases:
        stop = start + bias.shape[0]
        for at in range(0, HW, HD):
            scores = dot(
                keys[at : at + HD, start:stop].astype(jnp.bfloat16),
                query[at : at + HD, start:stop].astype(jnp.bfloat16),
                COLUMNS_BY_COLUMNS,
            )
            scores = scores * SCALE + bias
            weight = jnp.exp2(scores - jnp.max(scores, axis=0, keepdims=True))
            total = jnp.sum(weight, axis=0, keepdims=True)
            probs.append((weight.astype(jnp.bfloat16), 1.0 / total))
        start = stop
    values = dot(w_v(), normed, ROWS_BY_ROWS)
    attn = []
    start = 0
    for index, bias in enumerate(biases):
        stop = start + bias.shape[0]
        heads = []
        for head in range(HEADS):
            at = head * HD
            weight, share = probs[index * HEADS + head]
            part = values[at : at + HD, start:stop].astype(jnp.bfloat16)
            heads.append(jnp.dot(part, weight, preferred_element_type=jnp.float32) * share)
        attn.append(jnp.concatenate(heads, axis=0))
        start = stop
    attn = jnp.concatenate(attn, axis=1).astype(jnp.bfloat16)
    block = rows.astype(jnp.float32) + dot(attn, w_out(), COLUMNS_BY_COLUMNS)
    return block.astype(jnp.bfloat16)


def iotas(size):
    return (
        lax.broadcasted_iota(jnp.int32, (size, size), 0),
        lax.broadcasted_iota(jnp.int32, (size, size), 1),
    )


def streamed(w_qkv, w_out, proj, back, sems):
    copies = [
        pltpu.make_async_copy(w_qkv.at[pl.ds(part * HW, HW)], proj.at[part], sems.at[part])
        for part in range(3)
    ]
    copies.append(pltpu.make_async_copy(w_out, back, sems.at[3]))

    def reader(part):
        def read():
            for copy in {0: copies[:1], 1: copies[1:]}.get(part, []):
                copy.wait()
            return proj[part] if part < 3 else back[...]

        return read

    return copies, [reader(part) for part in range(4)]


def spatial_kernel(clips, slots, slen, x, w_qkv, w_out, out, proj, back, sems, own):
    copies, weights = streamed(w_qkv, w_out, proj, back, sems)
    arrival = pltpu.make_async_copy(x, own, sems.at[4])
    arrival.start()
    copies[0].start()
    group = lax.axis_index("dp")
    total = clips * slots
    biases = []
    for start in range(0, total, BLOCK):
        size = min(BLOCK, total - start)
        row, col = iotas(size)
        live = jnp.zeros((size, size), jnp.bool_)
        for clip in range(start // slots, (start + size) // slots):
            first = clip * slots - start
            live = live | (
                (col >= first)
                & (col < first + slots)
                & (row >= first)
                & (row < first + slen[group * clips + clip])
            )
        biases.append(jnp.where(live, 0.0, -1e30))
    out[total:] = jnp.zeros((out.shape[0] - total, out.shape[1]), jnp.bfloat16)
    arrival.wait()
    for copy in copies[1:]:
        copy.start()
    out[:total] = attention_part(own[...], *weights, biases)


def temporal_kernel(
    clips, slots, groups, frames, each, flen, target, x, w_qkv, w_out, out, proj, back, sems
):
    copies, weights = streamed(w_qkv, w_out, proj, back, sems)
    for copy in copies:
        copy.start()
    home = lax.axis_index("seq") * groups + lax.axis_index("dp")
    slot = jnp.minimum(home * each // slots, clips - 1)
    plane = groups * each
    row, col = iotas(plane)
    goal = jnp.zeros((plane, plane), jnp.int32)
    most = jnp.zeros((plane, plane), jnp.int32)
    for group in range(groups):
        here = col // each == group
        goal = jnp.where(here, target[group * clips + slot] // clips, goal)
        most = jnp.where(here, flen[group * clips + slot], most)
    moved = (goal == row // each) & (row % each == col % each)
    most = jnp.sum(jnp.where(moved, most.astype(jnp.float32), 0.0), axis=1, keepdims=True)
    moved = jnp.where(moved, 1.0, 0.0).astype(jnp.bfloat16)
    planes = [
        jnp.dot(
            moved, x[frame * plane : (frame + 1) * plane], preferred_element_type=jnp.float32
        ).astype(jnp.bfloat16)
        for frame in range(frames)
    ]
    part = BLOCK // frames
    starts = range(0, plane, part)
    row, col = iotas(BLOCK)
    same = row % part == col % part
    frame = (row // part).astype(jnp.float32)
    biases = []
    for start in starts:
        live = jnp.concatenate([most[start : start + part]] * frames, axis=0)
        biases.append(jnp.where(same & (frame < live), 0.0, -1e30))
    rows = jnp.concatenate([each[start : start + part] for start in starts for each in planes])
    block = attention_part(rows, *weights, biases)
    for index, start in enumerate(starts):
        for frame in range(frames):
            at = frame * plane + start
            first = index * BLOCK + frame * part
            out[at : at + part] = block[first : first + part]


def crop_kernel(pieces, x, out, sems):
    size = out.shape[0] // pieces
    copies = [
        pltpu.make_async_copy(
            x.at[pl.ds(piece * size, size)], out.at[pl.ds(piece * size, size)], sems.at[piece]
        )
        for piece in range(pieces)
    ]
    for copy in copies:
        copy.start()
    for copy in copies:
        copy.wait()


def per_device(
    latents,
    w_spatial_qkv,
    w_spatial_out,
    w_temporal_qkv,
    w_temporal_out,
    spatial_len,
    frames_len,
    target,
):
    clips, _, slots, width = latents.shape
    groups, frames = lax.axis_size("dp"), lax.axis_size("seq")
    devices = groups * frames
    each = -(-clips * slots // devices)
    rows = devices * each
    smem = pl.BlockSpec(memory_space=pltpu.SMEM)
    vmem = pl.BlockSpec(memory_space=pltpu.VMEM)
    hbm = pl.BlockSpec(memory_space=pl.ANY)

    def exchange(values):
        return lax.all_to_all(
            values.reshape(devices, each, width),
            ("seq", "dp"),
            split_axis=0,
            concat_axis=0,
            tiled=True,
        ).reshape(rows, width)

    def call(kernel, scalars, values, w_qkv, w_out, where, limit, extra):
        return pl.pallas_call(
            kernel,
            out_shape=pltpu.VMEM((rows, width), jnp.bfloat16),
            in_specs=[smem] * len(scalars) + [where, hbm, hbm],
            out_specs=vmem,
            scratch_shapes=[
                pltpu.VMEM((3, HW, width), jnp.bfloat16),
                pltpu.VMEM((HW, width), jnp.bfloat16),
                pltpu.SemaphoreType.DMA((5,)),
                *extra,
            ],
            compiler_params=pltpu.CompilerParams(vmem_limit_bytes=limit),
        )(*scalars, values, w_qkv.T, w_out)

    mid = call(
        functools.partial(spatial_kernel, clips, slots),
        [spatial_len],
        latents.reshape(clips * slots, width),
        w_spatial_qkv,
        w_spatial_out,
        hbm,
        55 * MIB,
        [pltpu.VMEM((clips * slots, width), jnp.bfloat16)],
    )
    block = call(
        functools.partial(temporal_kernel, clips, slots, groups, frames, each),
        [frames_len, target],
        exchange(mid),
        w_temporal_qkv,
        w_temporal_out,
        vmem,
        51 * MIB,
        [],
    )
    final = pl.pallas_call(
        functools.partial(crop_kernel, clips),
        out_shape=jax.ShapeDtypeStruct((clips * slots, width), jnp.bfloat16),
        in_specs=[hbm],
        out_specs=hbm,
        scratch_shapes=[pltpu.SemaphoreType.DMA((clips,))],
        compiler_params=pltpu.CompilerParams(vmem_limit_bytes=40 * MIB),
    )(exchange(block))
    return final.reshape(latents.shape)


def solution(mesh):
    return jax.shard_map(
        per_device,
        mesh=mesh,
        in_specs=(P("dp", "seq", None, None), P(), P(), P(), P(), P(), P(), P()),
        out_specs=P("dp", "seq", None, None),
        check_vma=False,
    )
```

```python
import functools

import jax
import jax.numpy as jnp
from jax import lax
from jax.experimental import pallas as pl
from jax.experimental.pallas import tpu as pltpu
from jax.sharding import PartitionSpec as P

HEADS = 8
HD = 72
HW = 576
BLOCK = 128
MIB = 1024 * 1024
ROWS_BY_ROWS = (((1,), (1,)), ((), ()))
COLUMNS_BY_COLUMNS = (((0,), (0,)), ((), ()))
SCALE = HD ** (-0.5) * 1.4426950408889634


def layer_norm(values):
    wide = values.astype(jnp.float32)
    centre = wide - jnp.mean(wide, axis=-1, keepdims=True)
    spread = jnp.mean(centre * centre, axis=-1, keepdims=True)
    return (centre * lax.rsqrt(spread + 1e-06)).astype(jnp.bfloat16)


def dot(left, right, dims):
    return lax.dot_general(left, right, dims, preferred_element_type=jnp.float32)


def attention_part(rows, w_q, w_k, w_v, w_out, biases):
    normed = layer_norm(rows)
    query = dot(w_q(), normed, ROWS_BY_ROWS)
    keys = dot(w_k(), normed, ROWS_BY_ROWS)
    probs = []
    start = 0
    for bias in biases:
        stop = start + bias.shape[0]
        for at in range(0, HW, HD):
            scores = dot(
                keys[at : at + HD, start:stop].astype(jnp.bfloat16),
                query[at : at + HD, start:stop].astype(jnp.bfloat16),
                COLUMNS_BY_COLUMNS,
            )
            scores = scores * SCALE + bias
            weight = jnp.exp2(scores - jnp.max(scores, axis=0, keepdims=True))
            total = jnp.sum(weight, axis=0, keepdims=True)
            probs.append((weight.astype(jnp.bfloat16), 1.0 / total))
        start = stop
    values = dot(w_v(), normed, ROWS_BY_ROWS)
    attn = []
    start = 0
    for index, bias in enumerate(biases):
        stop = start + bias.shape[0]
        heads = []
        for head in range(HEADS):
            at = head * HD
            weight, share = probs[index * HEADS + head]
            part = values[at : at + HD, start:stop].astype(jnp.bfloat16)
            heads.append(jnp.dot(part, weight, preferred_element_type=jnp.float32) * share)
        attn.append(jnp.concatenate(heads, axis=0))
        start = stop
    attn = jnp.concatenate(attn, axis=1).astype(jnp.bfloat16)
    block = rows.astype(jnp.float32) + dot(attn, w_out(), COLUMNS_BY_COLUMNS)
    return block.astype(jnp.bfloat16)


def iotas(size):
    return (
        lax.broadcasted_iota(jnp.int32, (size, size), 0),
        lax.broadcasted_iota(jnp.int32, (size, size), 1),
    )


def streamed(w_qkv, w_out, proj, back, sems):
    copies = [
        pltpu.make_async_copy(w_qkv.at[pl.ds(part * HW, HW)], proj.at[part], sems.at[part])
        for part in range(3)
    ]
    copies.append(pltpu.make_async_copy(w_out, back, sems.at[3]))

    def reader(part):
        def read():
            for copy in {0: copies[:1], 1: copies[1:]}.get(part, []):
                copy.wait()
            return proj[part] if part < 3 else back[...]

        return read

    return copies, [reader(part) for part in range(4)]


def spatial_kernel(clips, slots, slen, x, w_qkv, w_out, out, proj, back, sems, own):
    copies, weights = streamed(w_qkv, w_out, proj, back, sems)
    arrival = pltpu.make_async_copy(x, own, sems.at[4])
    arrival.start()
    copies[0].start()
    group = lax.axis_index("dp")
    total = clips * slots
    biases = []
    for start in range(0, total, BLOCK):
        size = min(BLOCK, total - start)
        row, col = iotas(size)
        live = jnp.zeros((size, size), jnp.bool_)
        for clip in range(start // slots, (start + size) // slots):
            first = clip * slots - start
            live = live | (
                (col >= first)
                & (col < first + slots)
                & (row >= first)
                & (row < first + slen[group * clips + clip])
            )
        biases.append(jnp.where(live, 0.0, -1e30))
    each, width = out.shape[1:]
    filled = total // each
    out[filled:] = jnp.zeros((out.shape[0] - filled, each, width), jnp.bfloat16)
    arrival.wait()
    for copy in copies[1:]:
        copy.start()
    block = attention_part(own[...], *weights, biases)
    out[:filled] = block.reshape(filled, each, width)


def temporal_kernel(
    clips, slots, groups, frames, each, flen, target, x, w_qkv, w_out, out, proj, back, sems
):
    copies, weights = streamed(w_qkv, w_out, proj, back, sems)
    for copy in copies:
        copy.start()
    home = lax.axis_index("seq") * groups + lax.axis_index("dp")
    slot = jnp.minimum(home * each // slots, clips - 1)
    plane = groups * each
    row, col = iotas(plane)
    goal = jnp.zeros((plane, plane), jnp.int32)
    most = jnp.zeros((plane, plane), jnp.int32)
    for group in range(groups):
        here = col // each == group
        goal = jnp.where(here, target[group * clips + slot] // clips, goal)
        most = jnp.where(here, flen[group * clips + slot], most)
    moved = (goal == row // each) & (row % each == col % each)
    most = jnp.sum(jnp.where(moved, most.astype(jnp.float32), 0.0), axis=1, keepdims=True)
    moved = jnp.where(moved, 1.0, 0.0).astype(jnp.bfloat16)
    planes = [
        jnp.dot(
            moved,
            x[frame * groups : (frame + 1) * groups].reshape(plane, x.shape[2]),
            preferred_element_type=jnp.float32,
        ).astype(jnp.bfloat16)
        for frame in range(frames)
    ]
    part = BLOCK // frames
    starts = range(0, plane, part)
    row, col = iotas(BLOCK)
    same = row % part == col % part
    frame = (row // part).astype(jnp.float32)
    biases = []
    for start in starts:
        live = jnp.concatenate([most[start : start + part]] * frames, axis=0)
        biases.append(jnp.where(same & (frame < live), 0.0, -1e30))
    rows = jnp.concatenate([held[start : start + part] for start in starts for held in planes])
    block = attention_part(rows, *weights, biases)
    for index, start in enumerate(starts):
        for frame in range(frames):
            at = (frame * plane + start) // each
            first = index * BLOCK + frame * part
            out[at : at + part // each] = block[first : first + part].reshape(
                part // each, each, block.shape[1]
            )


def crop_kernel(pieces, x, out, rows, sems):
    size, width = out.shape[0] // pieces, out.shape[1]
    chunk = size // x.shape[1]
    copies = []
    for piece in range(pieces):
        span = pl.ds(piece * size, size)
        rows[piece * size : (piece + 1) * size] = x[piece * chunk : (piece + 1) * chunk].reshape(
            size, width
        )
        copies.append(pltpu.make_async_copy(rows.at[span], out.at[span], sems.at[piece]))
        copies[-1].start()
    for copy in copies:
        copy.wait()


def per_device(
    latents,
    w_spatial_qkv,
    w_spatial_out,
    w_temporal_qkv,
    w_temporal_out,
    spatial_len,
    frames_len,
    target,
):
    clips, _, slots, width = latents.shape
    groups, frames = lax.axis_size("dp"), lax.axis_size("seq")
    devices = groups * frames
    each = -(-clips * slots // devices)
    smem = pl.BlockSpec(memory_space=pltpu.SMEM)
    vmem = pl.BlockSpec(memory_space=pltpu.VMEM)
    hbm = pl.BlockSpec(memory_space=pl.ANY)

    def exchange(values):
        return lax.all_to_all(
            values,
            ("seq", "dp"),
            split_axis=0,
            concat_axis=0,
            tiled=True,
        )

    def call(kernel, scalars, values, w_qkv, w_out, where, limit, extra):
        return pl.pallas_call(
            kernel,
            out_shape=pltpu.VMEM((devices, each, width), jnp.bfloat16),
            in_specs=[smem] * len(scalars) + [where, hbm, hbm],
            out_specs=vmem,
            scratch_shapes=[
                pltpu.VMEM((3, HW, width), jnp.bfloat16),
                pltpu.VMEM((HW, width), jnp.bfloat16),
                pltpu.SemaphoreType.DMA((5,)),
                *extra,
            ],
            compiler_params=pltpu.CompilerParams(vmem_limit_bytes=limit),
        )(*scalars, values, w_qkv.T, w_out)

    mid = call(
        functools.partial(spatial_kernel, clips, slots),
        [spatial_len],
        latents.reshape(clips * slots, width),
        w_spatial_qkv,
        w_spatial_out,
        hbm,
        55 * MIB,
        [pltpu.VMEM((clips * slots, width), jnp.bfloat16)],
    )
    block = call(
        functools.partial(temporal_kernel, clips, slots, groups, frames, each),
        [frames_len, target],
        exchange(mid),
        w_temporal_qkv,
        w_temporal_out,
        vmem,
        51 * MIB,
        [],
    )
    final = pl.pallas_call(
        functools.partial(crop_kernel, clips),
        out_shape=jax.ShapeDtypeStruct((clips * slots, width), jnp.bfloat16),
        in_specs=[vmem],
        out_specs=hbm,
        scratch_shapes=[
            pltpu.VMEM((clips * slots, width), jnp.bfloat16),
            pltpu.SemaphoreType.DMA((clips,)),
        ],
        compiler_params=pltpu.CompilerParams(vmem_limit_bytes=40 * MIB),
    )(exchange(block))
    return final.reshape(latents.shape)


def solution(mesh):
    return jax.shard_map(
        per_device,
        mesh=mesh,
        in_specs=(P("dp", "seq", None, None), P(), P(), P(), P(), P(), P(), P()),
        out_specs=P("dp", "seq", None, None),
        check_vma=False,
    )
```

```python
import functools

import jax
import jax.numpy as jnp
from jax import lax
from jax.experimental import pallas as pl
from jax.experimental.pallas import tpu as pltpu
from jax.sharding import PartitionSpec as P

HEADS = 8
HD = 72
HW = 576
BLOCK = 128
MIB = 1024 * 1024
ROWS_BY_ROWS = (((1,), (1,)), ((), ()))
COLUMNS_BY_COLUMNS = (((0,), (0,)), ((), ()))
SCALE = HD ** (-0.5) * 1.4426950408889634


def layer_norm(values):
    wide = values.astype(jnp.float32)
    centre = wide - jnp.mean(wide, axis=-1, keepdims=True)
    spread = jnp.mean(centre * centre, axis=-1, keepdims=True)
    return (centre * lax.rsqrt(spread + 1e-06)).astype(jnp.bfloat16)


def dot(left, right, dims):
    return lax.dot_general(left, right, dims, preferred_element_type=jnp.float32)


def attention_part(rows, w_q, w_k, w_v, w_out, biases):
    normed = layer_norm(rows)
    query = dot(w_q(), normed, ROWS_BY_ROWS)
    keys = dot(w_k(), normed, ROWS_BY_ROWS)
    probs = []
    start = 0
    for bias in biases:
        stop = start + bias.shape[0]
        for at in range(0, HW, HD):
            scores = dot(
                keys[at : at + HD, start:stop].astype(jnp.bfloat16),
                query[at : at + HD, start:stop].astype(jnp.bfloat16),
                COLUMNS_BY_COLUMNS,
            )
            scores = scores * SCALE + bias
            weight = jnp.exp2(scores - jnp.max(scores, axis=0, keepdims=True))
            total = jnp.sum(weight, axis=0, keepdims=True)
            probs.append((weight.astype(jnp.bfloat16), 1.0 / total))
        start = stop
    values = dot(w_v(), normed, ROWS_BY_ROWS)
    attn = []
    start = 0
    for index, bias in enumerate(biases):
        stop = start + bias.shape[0]
        heads = []
        for head in range(HEADS):
            at = head * HD
            weight, share = probs[index * HEADS + head]
            part = values[at : at + HD, start:stop].astype(jnp.bfloat16)
            heads.append(jnp.dot(part, weight, preferred_element_type=jnp.float32) * share)
        attn.append(jnp.concatenate(heads, axis=0))
        start = stop
    attn = jnp.concatenate(attn, axis=1).astype(jnp.bfloat16)
    block = rows.astype(jnp.float32) + dot(attn, w_out(), COLUMNS_BY_COLUMNS)
    return block.astype(jnp.bfloat16)


def iotas(size):
    return (
        lax.broadcasted_iota(jnp.int32, (size, size), 0),
        lax.broadcasted_iota(jnp.int32, (size, size), 1),
    )


def streamed(w_qkv, w_out, proj, back, sems):
    copies = [
        pltpu.make_async_copy(w_qkv.at[pl.ds(part * HW, HW)], proj.at[part], sems.at[part])
        for part in range(3)
    ]
    copies.append(pltpu.make_async_copy(w_out, back, sems.at[3]))

    def reader(part):
        def read():
            for copy in {0: copies[:1], 1: copies[1:]}.get(part, []):
                copy.wait()
            return proj[part] if part < 3 else back[...]

        return read

    return copies, [reader(part) for part in range(4)]


def spatial_kernel(
    clips,
    slots,
    slen,
    x,
    w_qkv,
    w_out,
    next_qkv,
    next_out,
    out,
    kept_qkv,
    kept_out,
    proj,
    back,
    sems,
    own,
):
    copies, weights = streamed(w_qkv, w_out, proj, back, sems)
    arrival = pltpu.make_async_copy(x, own, sems.at[4])
    arrival.start()
    copies[0].start()
    group = lax.axis_index("dp")
    total = clips * slots
    biases = []
    for start in range(0, total, BLOCK):
        size = min(BLOCK, total - start)
        row, col = iotas(size)
        live = jnp.zeros((size, size), jnp.bool_)
        for clip in range(start // slots, (start + size) // slots):
            first = clip * slots - start
            live = live | (
                (col >= first)
                & (col < first + slots)
                & (row >= first)
                & (row < first + slen[group * clips + clip])
            )
        biases.append(jnp.where(live, 0.0, -1e30))
    each, width = out.shape[1:]
    filled = total // each
    out[filled:] = jnp.zeros((out.shape[0] - filled, each, width), jnp.bfloat16)
    arrival.wait()
    for copy in copies[1:]:
        copy.start()
    later = [
        pltpu.make_async_copy(next_qkv, kept_qkv, sems.at[5]),
        pltpu.make_async_copy(next_out, kept_out, sems.at[6]),
    ]

    def keys_weights():
        held = weights[1]()
        for copy in later:
            copy.start()
        return held

    block = attention_part(own[...], weights[0], keys_weights, *weights[2:], biases)
    out[:filled] = block.reshape(filled, each, width)
    for copy in later:
        copy.wait()


def temporal_kernel(
    clips, slots, groups, frames, each, flen, target, x, w_qkv, w_out, out
):
    home = lax.axis_index("seq") * groups + lax.axis_index("dp")
    slot = jnp.minimum(home * each // slots, clips - 1)
    plane = groups * each
    row, col = iotas(plane)
    goal = jnp.zeros((plane, plane), jnp.int32)
    most = jnp.zeros((plane, plane), jnp.int32)
    for group in range(groups):
        here = col // each == group
        goal = jnp.where(here, target[group * clips + slot] // clips, goal)
        most = jnp.where(here, flen[group * clips + slot], most)
    moved = (goal == row // each) & (row % each == col % each)
    most = jnp.sum(jnp.where(moved, most.astype(jnp.float32), 0.0), axis=1, keepdims=True)
    moved = jnp.where(moved, 1.0, 0.0).astype(jnp.bfloat16)
    planes = [
        jnp.dot(
            moved,
            x[frame * groups : (frame + 1) * groups].reshape(plane, x.shape[2]),
            preferred_element_type=jnp.float32,
        ).astype(jnp.bfloat16)
        for frame in range(frames)
    ]
    part = BLOCK // frames
    starts = range(0, plane, part)
    row, col = iotas(BLOCK)
    same = row % part == col % part
    frame = (row // part).astype(jnp.float32)
    biases = []
    for start in starts:
        live = jnp.concatenate([most[start : start + part]] * frames, axis=0)
        biases.append(jnp.where(same & (frame < live), 0.0, -1e30))
    rows = jnp.concatenate([held[start : start + part] for start in starts for held in planes])
    block = attention_part(
        rows,
        lambda: w_qkv[:HW],
        lambda: w_qkv[HW : 2 * HW],
        lambda: w_qkv[2 * HW :],
        lambda: w_out[...],
        biases,
    )
    for index, start in enumerate(starts):
        for frame in range(frames):
            at = (frame * plane + start) // each
            first = index * BLOCK + frame * part
            out[at : at + part // each] = block[first : first + part].reshape(
                part // each, each, block.shape[1]
            )


def crop_kernel(pieces, x, out, rows, sems):
    size, width = out.shape[0] // pieces, out.shape[1]
    chunk = size // x.shape[1]
    copies = []
    for piece in range(pieces):
        span = pl.ds(piece * size, size)
        rows[piece * size : (piece + 1) * size] = x[piece * chunk : (piece + 1) * chunk].reshape(
            size, width
        )
        copies.append(pltpu.make_async_copy(rows.at[span], out.at[span], sems.at[piece]))
        copies[-1].start()
    for copy in copies:
        copy.wait()


def per_device(
    latents,
    w_spatial_qkv,
    w_spatial_out,
    w_temporal_qkv,
    w_temporal_out,
    spatial_len,
    frames_len,
    target,
):
    clips, _, slots, width = latents.shape
    groups, frames = lax.axis_size("dp"), lax.axis_size("seq")
    devices = groups * frames
    each = -(-clips * slots // devices)
    smem = pl.BlockSpec(memory_space=pltpu.SMEM)
    vmem = pl.BlockSpec(memory_space=pltpu.VMEM)
    hbm = pl.BlockSpec(memory_space=pl.ANY)

    def exchange(values):
        return lax.all_to_all(
            values,
            ("seq", "dp"),
            split_axis=0,
            concat_axis=0,
            tiled=True,
        )

    shape = (devices, each, width)
    mid, w_qkv, w_out = pl.pallas_call(
        functools.partial(spatial_kernel, clips, slots),
        out_shape=[
            pltpu.VMEM(shape, jnp.bfloat16),
            pltpu.VMEM((3 * HW, width), jnp.bfloat16),
            pltpu.VMEM((HW, width), jnp.bfloat16),
        ],
        in_specs=[smem] + [hbm] * 5,
        out_specs=[vmem] * 3,
        scratch_shapes=[
            pltpu.VMEM((3, HW, width), jnp.bfloat16),
            pltpu.VMEM((HW, width), jnp.bfloat16),
            pltpu.SemaphoreType.DMA((7,)),
            pltpu.VMEM((clips * slots, width), jnp.bfloat16),
        ],
        compiler_params=pltpu.CompilerParams(vmem_limit_bytes=50 * MIB),
    )(
        spatial_len,
        latents.reshape(clips * slots, width),
        w_spatial_qkv.T,
        w_spatial_out,
        w_temporal_qkv.T,
        w_temporal_out,
    )
    block = pl.pallas_call(
        functools.partial(temporal_kernel, clips, slots, groups, frames, each),
        out_shape=pltpu.VMEM(shape, jnp.bfloat16),
        in_specs=[smem] * 2 + [vmem] * 3,
        out_specs=vmem,
        compiler_params=pltpu.CompilerParams(vmem_limit_bytes=40 * MIB),
    )(frames_len, target, exchange(mid), w_qkv, w_out)
    final = pl.pallas_call(
        functools.partial(crop_kernel, clips),
        out_shape=jax.ShapeDtypeStruct((clips * slots, width), jnp.bfloat16),
        in_specs=[vmem],
        out_specs=hbm,
        scratch_shapes=[
            pltpu.VMEM((clips * slots, width), jnp.bfloat16),
            pltpu.SemaphoreType.DMA((clips,)),
        ],
        compiler_params=pltpu.CompilerParams(vmem_limit_bytes=40 * MIB),
    )(exchange(block))
    return final.reshape(latents.shape)


def solution(mesh):
    return jax.shard_map(
        per_device,
        mesh=mesh,
        in_specs=(P("dp", "seq", None, None), P(), P(), P(), P(), P(), P(), P()),
        out_specs=P("dp", "seq", None, None),
        check_vma=False,
    )
```

```python
import functools

import jax
import jax.numpy as jnp
from jax import lax
from jax.experimental import pallas as pl
from jax.experimental.pallas import tpu as pltpu
from jax.sharding import PartitionSpec as P

HEADS = 8
HD = 72
HW = 576
BLOCK = 128
MIB = 1024 * 1024
ROWS_BY_ROWS = (((1,), (1,)), ((), ()))
COLUMNS_BY_COLUMNS = (((0,), (0,)), ((), ()))
SCALE = HD ** (-0.5) * 1.4426950408889634


def layer_norm(values):
    wide = values.astype(jnp.float32)
    centre = wide - jnp.mean(wide, axis=-1, keepdims=True)
    spread = jnp.mean(centre * centre, axis=-1, keepdims=True)
    return (centre * lax.rsqrt(spread + 1e-06)).astype(jnp.bfloat16)


def dot(left, right, dims):
    return lax.dot_general(left, right, dims, preferred_element_type=jnp.float32)


def attention_part(rows, w_q, w_k, w_v, w_out, biases):
    normed = layer_norm(rows)
    query = dot(w_q(), normed, ROWS_BY_ROWS)
    keys = dot(w_k(), normed, ROWS_BY_ROWS)
    probs = []
    start = 0
    for bias in biases:
        stop = start + bias.shape[0]
        for at in range(0, HW, HD):
            scores = dot(
                keys[at : at + HD, start:stop].astype(jnp.bfloat16),
                query[at : at + HD, start:stop].astype(jnp.bfloat16),
                COLUMNS_BY_COLUMNS,
            )
            scores = scores * SCALE + bias
            weight = jnp.exp2(scores - jnp.max(scores, axis=0, keepdims=True))
            total = jnp.sum(weight, axis=0, keepdims=True)
            probs.append((weight.astype(jnp.bfloat16), 1.0 / total))
        start = stop
    values = dot(w_v(), normed, ROWS_BY_ROWS)
    attn = []
    start = 0
    for index, bias in enumerate(biases):
        stop = start + bias.shape[0]
        heads = []
        for head in range(HEADS):
            at = head * HD
            weight, share = probs[index * HEADS + head]
            part = values[at : at + HD, start:stop].astype(jnp.bfloat16)
            heads.append(jnp.dot(part, weight, preferred_element_type=jnp.float32) * share)
        attn.append(jnp.concatenate(heads, axis=0))
        start = stop
    back = w_out()
    block = []
    start = 0
    for index in range(0, len(attn), 2):
        part = jnp.concatenate(attn[index : index + 2], axis=1).astype(jnp.bfloat16)
        stop = start + part.shape[1]
        wide = rows[start:stop].astype(jnp.float32) + dot(part, back, COLUMNS_BY_COLUMNS)
        block.append(wide.astype(jnp.bfloat16))
        start = stop
    return jnp.concatenate(block, axis=0)


def iotas(size):
    return (
        lax.broadcasted_iota(jnp.int32, (size, size), 0),
        lax.broadcasted_iota(jnp.int32, (size, size), 1),
    )


def streamed(w_qkv, w_out, proj, back, sems):
    copies = [
        pltpu.make_async_copy(w_qkv.at[pl.ds(part * HW, HW)], proj.at[part], sems.at[part])
        for part in range(3)
    ]
    copies.append(pltpu.make_async_copy(w_out, back, sems.at[3]))

    def reader(part):
        def read():
            copies[part].wait()
            return proj[part] if part < 3 else back[...]

        return read

    return copies, [reader(part) for part in range(4)]


def spatial_kernel(
    clips,
    slots,
    slen,
    x,
    w_qkv,
    w_out,
    next_qkv,
    next_out,
    out,
    kept_qkv,
    kept_out,
    proj,
    back,
    sems,
    own,
):
    copies, weights = streamed(w_qkv, w_out, proj, back, sems)
    arrival = pltpu.make_async_copy(x, own, sems.at[4])
    arrival.start()
    copies[0].start()
    group = lax.axis_index("dp")
    total = clips * slots
    biases = []
    for start in range(0, total, BLOCK):
        size = min(BLOCK, total - start)
        row, col = iotas(size)
        live = jnp.zeros((size, size), jnp.bool_)
        for clip in range(start // slots, (start + size) // slots):
            first = clip * slots - start
            live = live | (
                (col >= first)
                & (col < first + slots)
                & (row >= first)
                & (row < first + slen[group * clips + clip])
            )
        biases.append(jnp.where(live, 0.0, -1e30))
    each, width = out.shape[1:]
    filled = total // each
    out[filled:] = jnp.zeros((out.shape[0] - filled, each, width), jnp.bfloat16)
    arrival.wait()
    for copy in copies[1:]:
        copy.start()
    later = [
        pltpu.make_async_copy(next_qkv, kept_qkv, sems.at[5]),
        pltpu.make_async_copy(next_out, kept_out, sems.at[6]),
    ]

    def values_weights():
        held = weights[2]()
        for copy in later:
            copy.start()
        return held

    block = attention_part(own[...], *weights[:2], values_weights, weights[3], biases)
    out[:filled] = block.reshape(filled, each, width)
    for copy in later:
        copy.wait()


def temporal_kernel(
    clips, slots, groups, frames, each, flen, target, x, w_qkv, w_out, out
):
    home = lax.axis_index("seq") * groups + lax.axis_index("dp")
    slot = jnp.minimum(home * each // slots, clips - 1)
    plane = groups * each
    row, col = iotas(plane)
    owner = lax.broadcasted_iota(jnp.int32, (1, plane), 1) // each
    goal = jnp.zeros((1, plane), jnp.int32)
    most = jnp.zeros((1, plane), jnp.int32)
    for group in range(groups):
        here = owner == group
        goal = jnp.where(here, target[group * clips + slot] // clips, goal)
        most = jnp.where(here, flen[group * clips + slot], most)
    moved = (goal == row // each) & (row % each == col % each)
    most = jnp.sum(jnp.where(moved, most.astype(jnp.float32), 0.0), axis=1, keepdims=True)
    moved = jnp.where(moved, 1.0, 0.0).astype(jnp.bfloat16)
    planes = [
        jnp.dot(
            moved,
            x[frame * groups : (frame + 1) * groups].reshape(plane, x.shape[2]),
            preferred_element_type=jnp.float32,
        ).astype(jnp.bfloat16)
        for frame in range(frames)
    ]
    part = BLOCK // frames
    starts = range(0, plane, part)
    row, col = iotas(BLOCK)
    same = row % part == col % part
    frame = (row // part).astype(jnp.float32)
    biases = []
    for start in starts:
        live = jnp.concatenate([most[start : start + part]] * frames, axis=0)
        biases.append(jnp.where(same & (frame < live), 0.0, -1e30))
    rows = jnp.concatenate([held[start : start + part] for start in starts for held in planes])
    block = attention_part(
        rows,
        lambda: w_qkv[:HW],
        lambda: w_qkv[HW : 2 * HW],
        lambda: w_qkv[2 * HW :],
        lambda: w_out[...],
        biases,
    )
    for index, start in enumerate(starts):
        for frame in range(frames):
            at = (frame * plane + start) // each
            first = index * BLOCK + frame * part
            out[at : at + part // each] = block[first : first + part].reshape(
                part // each, each, block.shape[1]
            )


def crop_kernel(pieces, x, out, rows, sems):
    size, width = out.shape[0] // pieces, out.shape[1]
    chunk = size // x.shape[1]
    copies = []
    for piece in range(pieces):
        span = pl.ds(piece * size, size)
        rows[piece * size : (piece + 1) * size] = x[piece * chunk : (piece + 1) * chunk].reshape(
            size, width
        )
        copies.append(pltpu.make_async_copy(rows.at[span], out.at[span], sems.at[piece]))
        copies[-1].start()
    for copy in copies:
        copy.wait()


def per_device(
    latents,
    w_spatial_qkv,
    w_spatial_out,
    w_temporal_qkv,
    w_temporal_out,
    spatial_len,
    frames_len,
    target,
):
    clips, _, slots, width = latents.shape
    groups, frames = lax.axis_size("dp"), lax.axis_size("seq")
    devices = groups * frames
    each = -(-clips * slots // devices)
    smem = pl.BlockSpec(memory_space=pltpu.SMEM)
    vmem = pl.BlockSpec(memory_space=pltpu.VMEM)
    hbm = pl.BlockSpec(memory_space=pl.ANY)

    def exchange(values):
        return lax.all_to_all(
            values,
            ("seq", "dp"),
            split_axis=0,
            concat_axis=0,
            tiled=True,
        )

    shape = (devices, each, width)
    mid, w_qkv, w_out = pl.pallas_call(
        functools.partial(spatial_kernel, clips, slots),
        out_shape=[
            pltpu.VMEM(shape, jnp.bfloat16),
            pltpu.VMEM((3 * HW, width), jnp.bfloat16),
            pltpu.VMEM((HW, width), jnp.bfloat16),
        ],
        in_specs=[smem] + [hbm] * 5,
        out_specs=[vmem] * 3,
        scratch_shapes=[
            pltpu.VMEM((3, HW, width), jnp.bfloat16),
            pltpu.VMEM((HW, width), jnp.bfloat16),
            pltpu.SemaphoreType.DMA((7,)),
            pltpu.VMEM((clips * slots, width), jnp.bfloat16),
        ],
        compiler_params=pltpu.CompilerParams(vmem_limit_bytes=50 * MIB),
    )(
        spatial_len,
        latents.reshape(clips * slots, width),
        w_spatial_qkv.T,
        w_spatial_out,
        w_temporal_qkv.T,
        w_temporal_out,
    )
    block = pl.pallas_call(
        functools.partial(temporal_kernel, clips, slots, groups, frames, each),
        out_shape=pltpu.VMEM(shape, jnp.bfloat16),
        in_specs=[smem] * 2 + [vmem] * 3,
        out_specs=vmem,
        compiler_params=pltpu.CompilerParams(vmem_limit_bytes=40 * MIB),
    )(frames_len, target, exchange(mid), w_qkv, w_out)
    final = pl.pallas_call(
        functools.partial(crop_kernel, clips),
        out_shape=jax.ShapeDtypeStruct((clips * slots, width), jnp.bfloat16),
        in_specs=[vmem],
        out_specs=hbm,
        scratch_shapes=[
            pltpu.VMEM((clips * slots, width), jnp.bfloat16),
            pltpu.SemaphoreType.DMA((clips,)),
        ],
        compiler_params=pltpu.CompilerParams(vmem_limit_bytes=40 * MIB),
    )(exchange(block))
    return final.reshape(latents.shape)


def solution(mesh):
    return jax.shard_map(
        per_device,
        mesh=mesh,
        in_specs=(P("dp", "seq", None, None), P(), P(), P(), P(), P(), P(), P()),
        out_specs=P("dp", "seq", None, None),
        check_vma=False,
    )
```

```python
import functools

import jax
import jax.numpy as jnp
from jax import lax
from jax.experimental import pallas as pl
from jax.experimental.pallas import tpu as pltpu
from jax.sharding import PartitionSpec as P

HEADS = 8
HD = 72
HW = 576
BLOCK = 128
MIB = 1024 * 1024
ROWS_BY_ROWS = (((1,), (1,)), ((), ()))
COLUMNS_BY_COLUMNS = (((0,), (0,)), ((), ()))
SCALE = HD ** (-0.5) * 1.4426950408889634


def layer_norm(values):
    wide = values.astype(jnp.float32)
    centre = wide - jnp.mean(wide, axis=-1, keepdims=True)
    spread = jnp.mean(centre * centre, axis=-1, keepdims=True)
    return (centre * lax.rsqrt(spread + 1e-06)).astype(jnp.bfloat16)


def dot(left, right, dims):
    return lax.dot_general(left, right, dims, preferred_element_type=jnp.float32)


def attention_part(rows, w_q, w_k, w_v, w_out, biases):
    normed = layer_norm(rows)
    query = dot(w_q(), normed, ROWS_BY_ROWS)
    keys = dot(w_k(), normed, ROWS_BY_ROWS)
    probs = []
    start = 0
    for bias in biases:
        stop = start + bias.shape[0]
        for at in range(0, HW, HD):
            scores = dot(
                keys[at : at + HD, start:stop].astype(jnp.bfloat16),
                query[at : at + HD, start:stop].astype(jnp.bfloat16),
                COLUMNS_BY_COLUMNS,
            )
            scores = scores * SCALE + bias
            weight = jnp.exp2(scores - jnp.max(scores, axis=0, keepdims=True))
            total = jnp.sum(weight, axis=0, keepdims=True)
            probs.append((weight.astype(jnp.bfloat16), 1.0 / total))
        start = stop
    values = dot(w_v(), normed, ROWS_BY_ROWS)
    attn = []
    start = 0
    for index, bias in enumerate(biases):
        stop = start + bias.shape[0]
        heads = []
        for head in range(HEADS):
            at = head * HD
            weight, share = probs[index * HEADS + head]
            part = values[at : at + HD, start:stop].astype(jnp.bfloat16)
            heads.append(jnp.dot(part, weight, preferred_element_type=jnp.float32) * share)
        attn.append(jnp.concatenate(heads, axis=0))
        start = stop
    back = w_out()
    block = []
    start = 0
    for index in range(0, len(attn), 2):
        part = jnp.concatenate(attn[index : index + 2], axis=1).astype(jnp.bfloat16)
        stop = start + part.shape[1]
        wide = rows[start:stop].astype(jnp.float32) + dot(part, back, COLUMNS_BY_COLUMNS)
        block.append(wide.astype(jnp.bfloat16))
        start = stop
    return jnp.concatenate(block, axis=0)


def iotas(size):
    return (
        lax.broadcasted_iota(jnp.int32, (size, size), 0),
        lax.broadcasted_iota(jnp.int32, (size, size), 1),
    )


def streamed(w_qkv, w_out, proj, back, sems):
    copies = [
        pltpu.make_async_copy(w_qkv.at[pl.ds(part * HW, HW)], proj.at[part], sems.at[part])
        for part in range(3)
    ]
    copies.append(pltpu.make_async_copy(w_out, back, sems.at[3]))

    def reader(part):
        def read():
            copies[part].wait()
            return proj[part] if part < 3 else back[...]

        return read

    return copies, [reader(part) for part in range(4)]


def temporal_plan(clips, slots, groups, frames, each, flen, target, move, mask):
    home = lax.axis_index("seq") * groups + lax.axis_index("dp")
    slot = jnp.minimum(home * each // slots, clips - 1)
    plane = groups * each
    row, col = iotas(plane)
    owner = lax.broadcasted_iota(jnp.int32, (1, plane), 1) // each
    goal = jnp.zeros((1, plane), jnp.int32)
    most = jnp.zeros((1, plane), jnp.int32)
    for group in range(groups):
        here = owner == group
        goal = jnp.where(here, target[group * clips + slot] // clips, goal)
        most = jnp.where(here, flen[group * clips + slot], most)
    moved = (goal == row // each) & (row % each == col % each)
    most = jnp.sum(jnp.where(moved, most.astype(jnp.float32), 0.0), axis=1, keepdims=True)
    move[...] = jnp.where(moved, 1.0, 0.0).astype(jnp.bfloat16)
    part = BLOCK // frames
    starts = range(0, plane, part)
    row, col = iotas(BLOCK)
    same = row % part == col % part
    frame = (row // part).astype(jnp.float32)
    for index, start in enumerate(starts):
        live = jnp.concatenate([most[start : start + part]] * frames, axis=0)
        mask[index] = jnp.where(same & (frame < live), 0.0, -1e30)


def spatial_kernel(
    clips,
    slots,
    groups,
    frames,
    each,
    slen,
    flen,
    target,
    x,
    w_qkv,
    w_out,
    next_qkv,
    next_out,
    out,
    kept_qkv,
    kept_out,
    move,
    mask,
    proj,
    back,
    sems,
    own,
):
    copies, weights = streamed(w_qkv, w_out, proj, back, sems)
    arrival = pltpu.make_async_copy(x, own, sems.at[4])
    arrival.start()
    copies[0].start()
    group = lax.axis_index("dp")
    total = clips * slots
    biases = []
    for start in range(0, total, BLOCK):
        size = min(BLOCK, total - start)
        row, col = iotas(size)
        live = jnp.zeros((size, size), jnp.bool_)
        for clip in range(start // slots, (start + size) // slots):
            first = clip * slots - start
            live = live | (
                (col >= first)
                & (col < first + slots)
                & (row >= first)
                & (row < first + slen[group * clips + clip])
            )
        biases.append(jnp.where(live, 0.0, -1e30))
    width = out.shape[2]
    filled = total // each
    out[filled:] = jnp.zeros((out.shape[0] - filled, each, width), jnp.bfloat16)
    temporal_plan(clips, slots, groups, frames, each, flen, target, move, mask)
    arrival.wait()
    for copy in copies[1:]:
        copy.start()
    later = [
        pltpu.make_async_copy(next_qkv, kept_qkv, sems.at[5]),
        pltpu.make_async_copy(next_out, kept_out, sems.at[6]),
    ]

    def values_weights():
        held = weights[2]()
        for copy in later:
            copy.start()
        return held

    block = attention_part(own[...], *weights[:2], values_weights, weights[3], biases)
    out[:filled] = block.reshape(filled, each, width)
    for copy in later:
        copy.wait()


def temporal_kernel(groups, frames, each, x, w_qkv, w_out, move, mask, out):
    plane = groups * each
    part = BLOCK // frames
    starts = range(0, plane, part)
    moved = move[...]
    biases = [mask[index] for index in range(len(starts))]
    planes = [
        jnp.dot(
            moved,
            x[frame * groups : (frame + 1) * groups].reshape(plane, x.shape[2]),
            preferred_element_type=jnp.float32,
        ).astype(jnp.bfloat16)
        for frame in range(frames)
    ]
    rows = jnp.concatenate([held[start : start + part] for start in starts for held in planes])
    block = attention_part(
        rows,
        lambda: w_qkv[:HW],
        lambda: w_qkv[HW : 2 * HW],
        lambda: w_qkv[2 * HW :],
        lambda: w_out[...],
        biases,
    )
    for index, start in enumerate(starts):
        for frame in range(frames):
            at = (frame * plane + start) // each
            first = index * BLOCK + frame * part
            out[at : at + part // each] = block[first : first + part].reshape(
                part // each, each, block.shape[1]
            )


def crop_kernel(pieces, x, out, rows, sems):
    size, width = out.shape[0] // pieces, out.shape[1]
    chunk = size // x.shape[1]
    copies = []
    for piece in range(pieces):
        span = pl.ds(piece * size, size)
        rows[piece * size : (piece + 1) * size] = x[piece * chunk : (piece + 1) * chunk].reshape(
            size, width
        )
        copies.append(pltpu.make_async_copy(rows.at[span], out.at[span], sems.at[piece]))
        copies[-1].start()
    for copy in copies:
        copy.wait()


def per_device(
    latents,
    w_spatial_qkv,
    w_spatial_out,
    w_temporal_qkv,
    w_temporal_out,
    spatial_len,
    frames_len,
    target,
):
    clips, _, slots, width = latents.shape
    groups, frames = lax.axis_size("dp"), lax.axis_size("seq")
    devices = groups * frames
    each = -(-clips * slots // devices)
    smem = pl.BlockSpec(memory_space=pltpu.SMEM)
    vmem = pl.BlockSpec(memory_space=pltpu.VMEM)
    hbm = pl.BlockSpec(memory_space=pl.ANY)

    def exchange(values):
        return lax.all_to_all(
            values,
            ("seq", "dp"),
            split_axis=0,
            concat_axis=0,
            tiled=True,
        )

    shape = (devices, each, width)
    mid, w_qkv, w_out, move, mask = pl.pallas_call(
        functools.partial(spatial_kernel, clips, slots, groups, frames, each),
        out_shape=[
            pltpu.VMEM(shape, jnp.bfloat16),
            pltpu.VMEM((3 * HW, width), jnp.bfloat16),
            pltpu.VMEM((HW, width), jnp.bfloat16),
            pltpu.VMEM((groups * each, groups * each), jnp.bfloat16),
            pltpu.VMEM((groups * each * frames // BLOCK, BLOCK, BLOCK), jnp.float32),
        ],
        in_specs=[smem] * 3 + [hbm] * 5,
        out_specs=[vmem] * 5,
        scratch_shapes=[
            pltpu.VMEM((3, HW, width), jnp.bfloat16),
            pltpu.VMEM((HW, width), jnp.bfloat16),
            pltpu.SemaphoreType.DMA((7,)),
            pltpu.VMEM((clips * slots, width), jnp.bfloat16),
        ],
        compiler_params=pltpu.CompilerParams(vmem_limit_bytes=50 * MIB),
    )(
        spatial_len,
        frames_len,
        target,
        latents.reshape(clips * slots, width),
        w_spatial_qkv.T,
        w_spatial_out,
        w_temporal_qkv.T,
        w_temporal_out,
    )
    block = pl.pallas_call(
        functools.partial(temporal_kernel, groups, frames, each),
        out_shape=pltpu.VMEM(shape, jnp.bfloat16),
        in_specs=[vmem] * 5,
        out_specs=vmem,
        compiler_params=pltpu.CompilerParams(vmem_limit_bytes=40 * MIB),
    )(exchange(mid), w_qkv, w_out, move, mask)
    final = pl.pallas_call(
        functools.partial(crop_kernel, clips),
        out_shape=jax.ShapeDtypeStruct((clips * slots, width), jnp.bfloat16),
        in_specs=[vmem],
        out_specs=hbm,
        scratch_shapes=[
            pltpu.VMEM((clips * slots, width), jnp.bfloat16),
            pltpu.SemaphoreType.DMA((clips,)),
        ],
        compiler_params=pltpu.CompilerParams(vmem_limit_bytes=40 * MIB),
    )(exchange(block))
    return final.reshape(latents.shape)


def solution(mesh):
    return jax.shard_map(
        per_device,
        mesh=mesh,
        in_specs=(P("dp", "seq", None, None), P(), P(), P(), P(), P(), P(), P()),
        out_specs=P("dp", "seq", None, None),
        check_vma=False,
    )
```
